512 devices in a mesh: pair: 64 (over z_lo, y, core), virt: 8 (over z_hi, x).
Axes of the slice: x: 4, y: 8, z: 8 (z_hi: 2, z_lo: 4; z = z_hi * 4 + z_lo), core: 2. Of those that a mesh axis runs over, the one named last changes fastest.
Arguments:
- amplitudes: bfloat16 [16384, 8192], P('pair', 'virt'), may hold values from -6 to 6
- amp_mask: int32 [16384, 64], P('pair', 'virt'), may hold values 0 or 1
- integrals: bfloat16 [64, 12, 128, 128], P('virt'), may hold values from -0.15625 to 0.15625
- int_rows: int32 [64, 12], P('virt'), may hold values from 0 to 63, all different within a row
- mirror_slot: int32 [4096, 4], P('pair'), may hold values from 0 to 3, each once within a row
Outputs:
- symmetric: bfloat16 [16384, 8192], P('pair', 'virt')
The draws below stay inside these ranges and needn't reach their ends.
Inputs may be any that keep to these rules, and one draw needn't show every extreme that they name: `int_rows`: each row names 12 different input tiles, and every input tile is named by some row. `mirror_slot`: each row is a permutation of 0 to 3.
All inputs are finite; a program needn't handle non-finite values. No bound on the sum of `amp_mask` on one device may be relied on, other than what follows from the above.
Results may differ from the reference program's by a relative error of at most 0.0051.
Values may be sent and summed in bfloat16 or wider, within the bound.
A program may use at most 128 MiB of HBM per device.

```python
import jax
import jax.numpy as jnp
from jax import lax

TILE = 128
PAIR_DEV = 256
NQ = 64
NP = 64
DEG = 12
PAIRS = 16384
BLK = 4
N_PAIR = 64


def plant(array, own_key, smallest, top_value):
    index_at = [jax.random.randint(jax.random.fold_in(own_key, axis), (), 0, length) for axis, length in enumerate(array.shape)]
    main_axis = array.shape.index(max(array.shape))
    beside = index_at[:main_axis] + [(index_at[main_axis] + 1) % array.shape[main_axis]] + index_at[main_axis + 1:]
    return array.at[tuple(index_at)].set(smallest).at[tuple(beside)].set(top_value)


def level_of(key, extent, pieces, least, high):
    def one(dim, parts):
        draws = jax.random.uniform(jax.random.fold_in(jax.random.fold_in(key, 6), dim), (parts,), jnp.float32, least / len(pieces), high / len(pieces))
        return jnp.repeat(jnp.exp(draws), extent[dim] // parts).reshape((-1,) + (1,) * (len(extent) - dim - 1))

    loudness = one(*pieces[0])
    for cut in pieces[1:]:
        loudness = loudness * one(*cut)
    return loudness


def choose_distinct(rng, rows, number_of, top, lift):
    ranking = jax.random.permutation(jax.random.fold_in(rng, 1), number_of)
    favour = ranking
    for power in range(3):
        favour = favour * favour // number_of
    favour = favour * lift // number_of
    chance = jax.random.randint(jax.random.fold_in(rng, 2), (rows, number_of), 0, 4096) + favour
    holders = jax.random.permutation(jax.random.fold_in(rng, 3), rows)[jnp.arange(number_of) % rows]
    chance = jnp.where(jnp.arange(rows)[:, None] == holders[None, :], 1 << 14, chance)
    priority = chance * number_of + jnp.arange(number_of)
    return lax.top_k(priority.astype(jnp.int32), top)[1].astype(jnp.int32)


def normal_values(stream_key, dims, spread, most, split=(), kind=jnp.bfloat16):
    array = spread * jax.random.normal(stream_key, dims, jnp.float32)
    if split:
        array = array * level_of(stream_key, dims, split, -0.22, 0.18)
    return jnp.clip(array, -most, most).astype(kind)


def setup_inputs(seed: int = 0) -> dict:
    key_of = jax.random.split(jax.random.key(seed), 6)
    amplitudes = normal_values(key_of[0], (PAIRS, NQ * TILE), 1.0, 6.0, ((0, 64), (1, 8)))
    amp_mask = plant((jax.random.randint(key_of[1], (PAIRS, NQ), 0, 4) < 3).astype(jnp.int32), jax.random.fold_in(key_of[1], 1), 0, 1)
    integrals = normal_values(key_of[2], (NP, DEG, TILE, TILE), (DEG * TILE) ** -0.5, 0.15625, ((0, 8),))
    int_rows = choose_distinct(key_of[3], NP, NQ, DEG, 1536)
    mirror_slot = jax.vmap(lambda own: jax.random.permutation(own, BLK))(jax.random.split(key_of[4], (N_PAIR * N_PAIR))).reshape((N_PAIR * N_PAIR, BLK)).astype(jnp.int32)
    return {"amplitudes": amplitudes, "amp_mask": amp_mask, "integrals": integrals, "int_rows": int_rows, "mirror_slot": mirror_slot}


def dense_integrals(integrals, int_rows):
    onehot = (int_rows[:, :, None] == jnp.arange(NQ, dtype=jnp.int32)[None, None, :]).astype(jnp.float32)
    dense = jnp.einsum("pkq,pkxy->qxpy", onehot, integrals.astype(jnp.float32))
    return dense.astype(jnp.bfloat16).reshape(NQ * TILE, NP * TILE)


def reference(amplitudes, amp_mask, integrals, int_rows, mirror_slot):
    dense = dense_integrals(integrals, int_rows)
    masked = (amplitudes.reshape(PAIRS, NQ, TILE) * amp_mask[:, :, None].astype(jnp.bfloat16)).reshape(PAIRS, NQ * TILE)

    def ladder_block(rows_block):
        return jnp.dot(rows_block, dense, preferred_element_type=jnp.float32).astype(jnp.bfloat16)

    ladder = lax.map(ladder_block, masked.reshape(N_PAIR, PAIR_DEV, NQ * TILE)).reshape(PAIRS, NP * TILE)
    device_ids = jnp.arange(N_PAIR, dtype=jnp.int32)
    slots = mirror_slot.reshape(N_PAIR, N_PAIR, BLK).astype(jnp.int32)
    mirror_rows = device_ids[None, :, None] * PAIR_DEV + device_ids[:, None, None] * BLK + slots
    mirrored = jnp.take(ladder, mirror_rows.reshape(PAIRS), axis=0)
    flipped = mirrored.reshape(PAIRS, NP, TILE)[:, :, ::-1].reshape(PAIRS, NP * TILE)
    return (ladder.astype(jnp.float32) + flipped.astype(jnp.float32)).astype(jnp.bfloat16)
```

```python
import jax
import jax.numpy as jnp
from jax import lax
from jax.experimental import pallas as pl
from jax.experimental.pallas import tpu as pltpu
from jax.sharding import PartitionSpec as P

MESH = pl.DeviceIdType.MESH
BF16, F32 = jnp.bfloat16, jnp.float32

TILE = 128
Q_LOCAL, P_LOCAL, DEG = 8, 8, 12
NX, NZH, NZL, NY, NC = 4, 2, 4, 8, 2
PEERS = NY * NC
BLK = 4
CHUNKS = NZL
ROWS = PEERS * BLK
HALF = 8
GROUP = HALF * BLK * P_LOCAL
PACK = P_LOCAL * BLK


def remote(src, dst, send, recv, to):
    return pltpu.make_async_remote_copy(
        src_ref=src, dst_ref=dst, send_sem=send, recv_sem=recv, device_id=to, device_id_type=MESH
    )


def kernel(
    amp_hbm, mask_hbm, int_hbm, rows_hbm, slot_hbm, out_hbm,
    x0, x1, x2, x3, lad, sent, got, amp, mask, weights, rows, slot, turn, swap, out,
    slot_wide, load_sem, store_sem, gs, gr, ms, mr, met,
):
    xs = (x0, x1, x2, x3)
    pair, virt = lax.axis_index("pair"), lax.axis_index("virt")
    zl, mine = pair // PEERS, lax.rem(pair, PEERS)
    y, core = mine // NC, lax.rem(mine, NC)
    zh, x = virt // NX, lax.rem(virt, NX)
    xr, xl, xo = lax.rem(x + 1, NX), lax.rem(x + 3, NX), lax.rem(x + 2, NX)
    zo = 1 - zh
    to_r, to_l, to_z = (pair, zh * NX + xr), (pair, zh * NX + xl), (pair, zo * NX + x)

    def flipped(k):
        return (zl, zl + 1 - 2 * lax.rem(zl, 2), lax.rem(zl + 2, 4), 3 - zl)[k]

    order = (3, 2, 1, 0)
    targets = [flipped(k) for k in order]

    barrier = pltpu.get_barrier_semaphore()
    y_peers = [(zl * PEERS + lax.rem(y + i, NY) * NC + core, virt) for i in range(1, NY)]
    z_peers = [
        (lax.rem(zl + i // NC, NZL) * PEERS + y * NC + lax.rem(core + i % NC, NC), virt)
        for i in range(1, NZL * NC)
    ]
    first = [to_r, to_l, to_z] + z_peers + y_peers
    for peer in first:
        pl.semaphore_signal(barrier, inc=1, device_id=peer, device_id_type=MESH)

    loads = [pltpu.make_async_copy(mask_hbm, mask, load_sem.at[0])]
    for n, target in enumerate(targets):
        part = pl.ds(pl.multiple_of(target * ROWS, ROWS), ROWS)
        loads.append(pltpu.make_async_copy(amp_hbm.at[part], amp.at[n], load_sem.at[1 + n]))
    loads.append(pltpu.make_async_copy(slot_hbm, slot, load_sem.at[5]))
    loads.append(pltpu.make_async_copy(rows_hbm, rows, load_sem.at[6]))
    loads.append(pltpu.make_async_copy(int_hbm, weights, load_sem.at[7]))
    for load in loads:
        load.start()

    pending = []

    def gather(n, i, first_tile, tiles):
        block = xs[n].at[pl.ds(first_tile, tiles)]
        return block, gs.at[n, i], gr.at[n, i]

    def send(n, i, first_tile, tiles, to):
        block, s, r = gather(n, i, first_tile, tiles)
        copy = remote(block, block, s, r, to)
        copy.start()
        pending.append(copy)

    def arrived(n, i, first_tile, tiles):
        block, s, r = gather(n, i, first_tile, tiles)
        remote(block, block, s, r, to_z).wait_recv()

    def tile(z_hi, at_x):
        return (z_hi * NX + at_x) * Q_LOCAL

    own, other = tile(zh, x), tile(zo, x)

    def masked(n):
        loads[1 + n].wait()
        part = pl.ds(pl.multiple_of(targets[n] * ROWS, ROWS), ROWS)
        keep = mask[part, :].astype(F32)
        for q in range(Q_LOCAL):
            a = amp[n, :, q * TILE : (q + 1) * TILE].astype(F32)
            xs[n][own + q] = (a * keep[:, q : q + 1]).astype(BF16)

    loads[0].wait()
    masked(0)
    pl.semaphore_wait(barrier, len(first))
    for n in range(CHUNKS):
        if n:
            masked(n)
        send(n, 2, own, Q_LOCAL, to_z)
        send(n, 0, own, Q_LOCAL, to_r)
        send(n, 1, own, Q_LOCAL, to_l)
    for peer in y_peers:
        pl.semaphore_signal(met, inc=1, device_id=peer, device_id_type=MESH)

    def grid(shape, axis):
        return lax.broadcasted_iota(jnp.int32, shape, axis)

    i, j = grid((GROUP, GROUP), 0), grid((GROUP, GROUP), 1)
    to_send = lax.rem(i // BLK, P_LOCAL) * (HALF * BLK) + (i // PACK) * BLK + lax.rem(i, BLK)
    turn[...] = jnp.where(j == to_send, 1.0, 0.0).astype(BF16)
    i, j = grid((TILE, TILE), 0), grid((TILE, TILE), 1)
    back = jnp.where(i + j == TILE - 1, 1.0, 0.0).astype(BF16)
    loads[5].wait()
    total = NZL * ROWS
    i, j = grid((total, NZL * PEERS), 0), grid((total, NZL * PEERS), 1)
    spread = jnp.where(i // BLK == j, 1.0, 0.0).astype(BF16)
    each = jnp.dot(spread, slot[...].astype(F32).astype(BF16), preferred_element_type=F32)
    i, j = grid((total, BLK), 0), grid((total, BLK), 1)
    column = jnp.sum(jnp.where(lax.rem(i, BLK) == j, each, 0.0), axis=1, keepdims=True)
    slot_wide[...] = jnp.broadcast_to(column, (total, TILE))
    for n in range(CHUNKS):
        for h in range(2):
            start = pl.multiple_of(targets[n] * ROWS + h * HALF * BLK, HALF * BLK)
            part = slot_wide[pl.ds(start, HALF * BLK), :]
            for half in range(2):
                i, j = grid((HALF * BLK, TILE), 0), grid((HALF * BLK, TILE), 1)
                offset = (j + half * TILE - (i // BLK) * PACK).astype(F32) - part
                for p in range(P_LOCAL):
                    swap[n, h, p * HALF * BLK : (p + 1) * HALF * BLK, half * TILE : (half + 1) * TILE] = (
                        jnp.where(offset == float(p * BLK), 1.0, 0.0).astype(BF16)
                    )
    loads[6].wait()
    loads[7].wait()

    def ladder(n):
        def one(p, carry):
            left = jnp.concatenate([xs[n][rows[p, k]] for k in range(DEG)], axis=1)
            acc = jnp.dot(left, weights[p], preferred_element_type=F32).astype(BF16)
            at = pl.ds(pl.multiple_of(p * HALF * BLK, HALF * BLK), HALF * BLK)
            lad[n, 0, at, :] = acc[: HALF * BLK]
            lad[n, 1, at, :] = acc[HALF * BLK :]
            return carry

        lax.fori_loop(0, P_LOCAL, one, 0)
        for h in range(2):
            packed = jnp.dot(turn[...], lad[n, h], preferred_element_type=F32).astype(BF16)
            sent[n, h * HALF : (h + 1) * HALF] = packed.reshape(HALF, PACK, TILE)

    def exchange(n):
        if order[n]:
            for i in range(PEERS):
                peer = (targets[n] * PEERS + i, virt)
                remote(sent.at[n, i], got.at[n, mine], ms.at[n], mr.at[n], peer).start()
        else:
            for i in range(1, PEERS):
                at = lax.rem(mine + i, PEERS)
                peer = (zl * PEERS + at, virt)
                remote(sent.at[n, at], got.at[n, mine], ms.at[n], mr.at[n], peer).start()
            got[n, mine] = sent[n, mine]

    def bytes_of(n):
        count = PEERS if order[n] else PEERS - 1
        part = pl.ds(0, count)
        return remote(sent.at[n, part], got.at[n, part], ms.at[n], mr.at[n], to_z)

    def combine(n):
        bytes_of(n).wait_recv()
        for h in range(2):
            block = got[n, h * HALF : (h + 1) * HALF].reshape(GROUP, TILE)
            mirrored = jnp.dot(swap[n, h], block, preferred_element_type=F32).astype(BF16)
            mirrored = jnp.dot(mirrored, back, preferred_element_type=F32)
            both = (lad[n, h].astype(F32) + mirrored).astype(BF16)
            for p in range(P_LOCAL):
                out[n, h * HALF * BLK : (h + 1) * HALF * BLK, p * TILE : (p + 1) * TILE] = (
                    both[p * HALF * BLK : (p + 1) * HALF * BLK]
                )
        part = pl.ds(pl.multiple_of(targets[n] * ROWS, ROWS), ROWS)
        pltpu.make_async_copy(out.at[n], out_hbm.at[part], store_sem.at[n]).start()

    for n in range(CHUNKS):
        arrived(n, 0, tile(zh, xl), 8)
        send(n, 3, tile(zh, xl), 4, to_r)
        arrived(n, 1, tile(zh, xr), 8)
        send(n, 4, tile(zh, xr) + 4, 4, to_l)
    for n in range(CHUNKS):
        arrived(n, 2, other, 8)
        send(n, 5, other, 8, to_r)
        send(n, 6, other, 8, to_l)
    pl.semaphore_wait(met, len(y_peers))

    def forward(n):
        arrived(n, 5, tile(zo, xl), 8)
        send(n, 7, tile(zo, xl), 4, to_r)
        arrived(n, 6, tile(zo, xr), 8)
        send(n, 8, tile(zo, xr) + 4, 4, to_l)

    def complete(n):
        arrived(n, 3, tile(zh, xo), 4)
        arrived(n, 4, tile(zh, xo) + 4, 4)
        arrived(n, 7, tile(zo, xo), 4)
        arrived(n, 8, tile(zo, xo) + 4, 4)

    forward(0)
    for n in range(CHUNKS):
        if n + 1 < CHUNKS:
            forward(n + 1)
        complete(n)
        ladder(n)
        exchange(n)
    for copy in pending:
        copy.wait_send()
    for n in range(CHUNKS):
        combine(n)
    for n in range(CHUNKS):
        bytes_of(n).wait_send()
        part = pl.ds(pl.multiple_of(targets[n] * ROWS, ROWS), ROWS)
        pltpu.make_async_copy(out.at[n], out_hbm.at[part], store_sem.at[n]).wait()


def on_device(amplitudes, amp_mask, integrals, int_rows, mirror_slot):
    hbm = pl.BlockSpec(memory_space=pl.ANY)
    total = CHUNKS * ROWS
    return pl.pallas_call(
        kernel,
        out_shape=jax.ShapeDtypeStruct((total, P_LOCAL * TILE), BF16),
        in_specs=[hbm] * 5,
        out_specs=hbm,
        scratch_shapes=[pltpu.VMEM((64, ROWS, TILE), BF16)] * CHUNKS
        + [
            pltpu.VMEM((CHUNKS, 2, GROUP, TILE), BF16),
            pltpu.VMEM((CHUNKS, PEERS, PACK, TILE), BF16),
            pltpu.VMEM((CHUNKS, PEERS, PACK, TILE), BF16),
            pltpu.VMEM((CHUNKS, ROWS, Q_LOCAL * TILE), BF16),
            pltpu.VMEM((total, Q_LOCAL), jnp.int32),
            pltpu.VMEM((P_LOCAL, DEG * TILE, TILE), BF16),
            pltpu.SMEM((P_LOCAL, DEG), jnp.int32),
            pltpu.VMEM((NZL * PEERS, BLK), jnp.int32),
            pltpu.VMEM((GROUP, GROUP), BF16),
            pltpu.VMEM((CHUNKS, 2, GROUP, GROUP), BF16),
            pltpu.VMEM((CHUNKS, ROWS, P_LOCAL * TILE), BF16),
            pltpu.VMEM((total, TILE), F32),
            pltpu.SemaphoreType.DMA((8,)),
            pltpu.SemaphoreType.DMA((CHUNKS,)),
            pltpu.SemaphoreType.DMA((CHUNKS, 9)),
            pltpu.SemaphoreType.DMA((CHUNKS, 9)),
            pltpu.SemaphoreType.DMA((CHUNKS,)),
            pltpu.SemaphoreType.DMA((CHUNKS,)),
            pltpu.SemaphoreType.REGULAR,
        ],
        compiler_params=pltpu.CompilerParams(
            collective_id=0, has_side_effects=True, vmem_limit_bytes=40 << 20
        ),
        name="ladder",
    )(amplitudes, amp_mask, integrals.reshape(P_LOCAL, DEG * TILE, TILE), int_rows, mirror_slot)


def solution(mesh):
    placed = (
        P("pair", "virt"),
        P("pair", "virt"),
        P("virt", None, None, None),
        P("virt", None),
        P("pair", None),
    )
    return jax.shard_map(
        on_device, mesh=mesh, in_specs=placed, out_specs=P("pair", "virt"), check_vma=False
    )
```

```python
import jax
import jax.numpy as jnp
from jax import lax
from jax.experimental import pallas as pl
from jax.experimental.pallas import tpu as pltpu
from jax.sharding import PartitionSpec as P

MESH = pl.DeviceIdType.MESH
BF16, F32 = jnp.bfloat16, jnp.float32

TILE = 128
Q_LOCAL, P_LOCAL, DEG = 8, 8, 12
NX, NZH, NZL, NY, NC = 4, 2, 4, 8, 2
PEERS = NY * NC
BLK = 4
CHUNKS = NZL
ROWS = PEERS * BLK
HALF = 8
GROUP = HALF * BLK * P_LOCAL
PACK = P_LOCAL * BLK


def remote(src, dst, send, recv, to):
    return pltpu.make_async_remote_copy(
        src_ref=src, dst_ref=dst, send_sem=send, recv_sem=recv, device_id=to, device_id_type=MESH
    )


def kernel(
    amp_hbm, mask_hbm, int_hbm, rows_hbm, slot_hbm, out,
    x0, x1, x2, x3, lad, sent, got, amp, mask, weights, rows, slot, turn, swap,
    slot_wide, keeps, load_sem, gs, gr, ms, mr, met,
):
    xs = (x0, x1, x2, x3)
    pair, virt = lax.axis_index("pair"), lax.axis_index("virt")
    zl, mine = pair // PEERS, lax.rem(pair, PEERS)
    y, core = mine // NC, lax.rem(mine, NC)
    zh, x = virt // NX, lax.rem(virt, NX)
    xr, xl, xo = lax.rem(x + 1, NX), lax.rem(x + 3, NX), lax.rem(x + 2, NX)
    zo = 1 - zh
    to_r, to_l, to_z = (pair, zh * NX + xr), (pair, zh * NX + xl), (pair, zo * NX + x)

    def flipped(k):
        return (zl, zl + 1 - 2 * lax.rem(zl, 2), lax.rem(zl + 2, 4), 3 - zl)[k]

    order = (3, 2, 1, 0)
    targets = [flipped(k) for k in order]

    barrier = pltpu.get_barrier_semaphore()
    y_peers = [(zl * PEERS + lax.rem(y + i, NY) * NC + core, virt) for i in range(1, NY)]
    z_peers = [
        (lax.rem(zl + i // NC, NZL) * PEERS + y * NC + lax.rem(core + i % NC, NC), virt)
        for i in range(1, NZL * NC)
    ]
    first = [to_r, to_l, to_z] + z_peers + y_peers
    for peer in first:
        pl.semaphore_signal(barrier, inc=1, device_id=peer, device_id_type=MESH)

    loads = [pltpu.make_async_copy(mask_hbm, mask, load_sem.at[0])]
    for n, target in enumerate(targets):
        part = pl.ds(pl.multiple_of(target * ROWS, ROWS), ROWS)
        loads.append(pltpu.make_async_copy(amp_hbm.at[part], amp.at[n], load_sem.at[1 + n]))
    loads.append(pltpu.make_async_copy(slot_hbm, slot, load_sem.at[5]))
    loads.append(pltpu.make_async_copy(rows_hbm, rows, load_sem.at[6]))
    loads.append(pltpu.make_async_copy(int_hbm, weights, load_sem.at[7]))
    for load in loads:
        load.start()

    pending = []

    def gather(n, i, first_tile, tiles):
        block = xs[n].at[pl.ds(first_tile, tiles)]
        return block, gs.at[n, i], gr.at[n, i]

    def send(n, i, first_tile, tiles, to):
        block, s, r = gather(n, i, first_tile, tiles)
        copy = remote(block, block, s, r, to)
        copy.start()
        pending.append(copy)

    def arrived(n, i, first_tile, tiles):
        block, s, r = gather(n, i, first_tile, tiles)
        remote(block, block, s, r, to_z).wait_recv()

    def tile(z_hi, at_x):
        return (z_hi * NX + at_x) * Q_LOCAL

    own, other = tile(zh, x), tile(zo, x)

    def masked(n):
        loads[1 + n].wait()
        part = pl.ds(pl.multiple_of(targets[n] * ROWS, ROWS), ROWS)
        keep = keeps[part, :]
        for q in range(Q_LOCAL):
            a = amp[n, :, q * TILE : (q + 1) * TILE].astype(F32)
            xs[n][own + q] = (a * keep[:, q : q + 1]).astype(BF16)

    loads[0].wait()
    keeps[...] = mask[...].astype(F32).T
    masked(0)
    pl.semaphore_wait(barrier, len(first))
    for n in range(CHUNKS):
        if n:
            masked(n)
        send(n, 2, own, Q_LOCAL, to_z)
        send(n, 0, own, Q_LOCAL, to_r)
        send(n, 1, own, Q_LOCAL, to_l)
    for peer in y_peers:
        pl.semaphore_signal(met, inc=1, device_id=peer, device_id_type=MESH)

    def grid(shape, axis):
        return lax.broadcasted_iota(jnp.int32, shape, axis)

    i, j = grid((GROUP, GROUP), 0), grid((GROUP, GROUP), 1)
    to_send = lax.rem(i // BLK, P_LOCAL) * (HALF * BLK) + (i // PACK) * BLK + lax.rem(i, BLK)
    turn[...] = jnp.where(j == to_send, 1.0, 0.0).astype(BF16)
    i, j = grid((TILE, TILE), 0), grid((TILE, TILE), 1)
    back = jnp.where(i + j == TILE - 1, 1.0, 0.0).astype(BF16)
    loads[5].wait()
    total = NZL * ROWS
    i, j = grid((total, NZL * PEERS), 0), grid((total, NZL * PEERS), 1)
    spread = jnp.where(i // BLK == j, 1.0, 0.0).astype(BF16)
    each = lax.dot_general(
        spread, slot[...].astype(F32).astype(BF16), (((1,), (1,)), ((), ())), preferred_element_type=F32
    )
    i, j = grid((total, BLK), 0), grid((total, BLK), 1)
    column = jnp.sum(jnp.where(lax.rem(i, BLK) == j, each, 0.0), axis=1, keepdims=True)
    slot_wide[...] = jnp.broadcast_to(column, (total, TILE))
    for n in range(CHUNKS):
        for h in range(2):
            start = pl.multiple_of(targets[n] * ROWS + h * HALF * BLK, HALF * BLK)
            part = slot_wide[pl.ds(start, HALF * BLK), :]
            for half in range(2):
                i, j = grid((HALF * BLK, TILE), 0), grid((HALF * BLK, TILE), 1)
                offset = (j + half * TILE - (i // BLK) * PACK).astype(F32) - part
                for p in range(P_LOCAL):
                    swap[n, h, p * HALF * BLK : (p + 1) * HALF * BLK, half * TILE : (half + 1) * TILE] = (
                        jnp.where(offset == float(p * BLK), 1.0, 0.0).astype(BF16)
                    )
    loads[6].wait()
    loads[7].wait()

    def ladder(n):
        def one(p, carry):
            left = jnp.concatenate([xs[n][rows[p, k]] for k in range(DEG)], axis=1)
            acc = jnp.dot(left, weights[p], preferred_element_type=F32).astype(BF16)
            at = pl.ds(pl.multiple_of(p * HALF * BLK, HALF * BLK), HALF * BLK)
            lad[n, 0, at, :] = acc[: HALF * BLK]
            lad[n, 1, at, :] = acc[HALF * BLK :]
            return carry

        lax.fori_loop(0, P_LOCAL, one, 0)
        for h in range(2):
            packed = jnp.dot(turn[...], lad[n, h], preferred_element_type=F32).astype(BF16)
            sent[n, h * HALF : (h + 1) * HALF] = packed.reshape(HALF, PACK, TILE)

    def exchange(n):
        if order[n]:
            for i in range(PEERS):
                peer = (targets[n] * PEERS + i, virt)
                remote(sent.at[n, i], got.at[n, mine], ms.at[n], mr.at[n], peer).start()
        else:
            for i in range(1, PEERS):
                at = lax.rem(mine + i, PEERS)
                peer = (zl * PEERS + at, virt)
                remote(sent.at[n, at], got.at[n, mine], ms.at[n], mr.at[n], peer).start()
            got[n, mine] = sent[n, mine]

    def bytes_of(n):
        count = PEERS if order[n] else PEERS - 1
        part = pl.ds(0, count)
        return remote(sent.at[n, part], got.at[n, part], ms.at[n], mr.at[n], to_z)

    def combine(n):
        bytes_of(n).wait_recv()
        for h in range(2):
            block = got[n, h * HALF : (h + 1) * HALF].reshape(GROUP, TILE)
            mirrored = jnp.dot(swap[n, h], block, preferred_element_type=F32).astype(BF16)
            mirrored = jnp.dot(mirrored, back, preferred_element_type=F32)
            both = (lad[n, h].astype(F32) + mirrored).astype(BF16)
            start = pl.multiple_of(targets[n] * ROWS + h * HALF * BLK, HALF * BLK)
            for p in range(P_LOCAL):
                out[pl.ds(start, HALF * BLK), p * TILE : (p + 1) * TILE] = both[
                    p * HALF * BLK : (p + 1) * HALF * BLK
                ]

    for n in range(CHUNKS):
        arrived(n, 0, tile(zh, xl), 8)
        send(n, 3, tile(zh, xl), 4, to_r)
        arrived(n, 1, tile(zh, xr), 8)
        send(n, 4, tile(zh, xr) + 4, 4, to_l)
    for n in range(CHUNKS):
        arrived(n, 2, other, 8)
        send(n, 5, other, 8, to_r)
        send(n, 6, other, 8, to_l)
    pl.semaphore_wait(met, len(y_peers))

    def forward(n):
        arrived(n, 5, tile(zo, xl), 8)
        send(n, 7, tile(zo, xl), 4, to_r)
        arrived(n, 6, tile(zo, xr), 8)
        send(n, 8, tile(zo, xr) + 4, 4, to_l)

    def complete(n):
        arrived(n, 3, tile(zh, xo), 4)
        arrived(n, 4, tile(zh, xo) + 4, 4)
        arrived(n, 7, tile(zo, xo), 4)
        arrived(n, 8, tile(zo, xo) + 4, 4)

    forward(0)
    for n in range(CHUNKS):
        if n + 1 < CHUNKS:
            forward(n + 1)
        complete(n)
        ladder(n)
        exchange(n)
    for copy in pending:
        copy.wait_send()
    for n in range(CHUNKS):
        combine(n)
    for n in range(CHUNKS):
        bytes_of(n).wait_send()


def on_device(amplitudes, amp_mask, integrals, int_rows, mirror_slot):
    hbm = pl.BlockSpec(memory_space=pl.ANY)
    total = CHUNKS * ROWS
    return pl.pallas_call(
        kernel,
        out_shape=pltpu.VMEM((total, P_LOCAL * TILE), BF16),
        in_specs=[hbm] * 5,
        out_specs=pl.BlockSpec(memory_space=pltpu.VMEM),
        scratch_shapes=[pltpu.VMEM((64, ROWS, TILE), BF16)] * CHUNKS
        + [
            pltpu.VMEM((CHUNKS, 2, GROUP, TILE), BF16),
            pltpu.VMEM((CHUNKS, PEERS, PACK, TILE), BF16),
            pltpu.VMEM((CHUNKS, PEERS, PACK, TILE), BF16),
            pltpu.VMEM((CHUNKS, ROWS, Q_LOCAL * TILE), BF16),
            pltpu.VMEM((Q_LOCAL, total), jnp.int32),
            pltpu.VMEM((P_LOCAL, DEG * TILE, TILE), BF16),
            pltpu.SMEM((P_LOCAL, DEG), jnp.int32),
            pltpu.VMEM((BLK, NZL * PEERS), jnp.int32),
            pltpu.VMEM((GROUP, GROUP), BF16),
            pltpu.VMEM((CHUNKS, 2, GROUP, GROUP), BF16),
            pltpu.VMEM((total, TILE), F32),
            pltpu.VMEM((total, Q_LOCAL), F32),
            pltpu.SemaphoreType.DMA((8,)),
            pltpu.SemaphoreType.DMA((CHUNKS, 9)),
            pltpu.SemaphoreType.DMA((CHUNKS, 9)),
            pltpu.SemaphoreType.DMA((CHUNKS,)),
            pltpu.SemaphoreType.DMA((CHUNKS,)),
            pltpu.SemaphoreType.REGULAR,
        ],
        compiler_params=pltpu.CompilerParams(
            collective_id=0, has_side_effects=True, vmem_limit_bytes=40 << 20
        ),
        name="ladder",
    )(
        *(
            pltpu.with_memory_space_constraint(a, pltpu.HBM)
            for a in (
                amplitudes,
                amp_mask.T,
                integrals.reshape(P_LOCAL, DEG * TILE, TILE),
                int_rows,
                mirror_slot.T,
            )
        )
    )


def solution(mesh):
    placed = (
        P("pair", "virt"),
        P("pair", "virt"),
        P("virt", None, None, None),
        P("virt", None),
        P("pair", None),
    )
    return jax.shard_map(
        on_device, mesh=mesh, in_specs=placed, out_specs=P("pair", "virt"), check_vma=False
    )
```

```python
import jax
import jax.numpy as jnp
from jax import lax
from jax.experimental import pallas as pl
from jax.experimental.pallas import tpu as pltpu
from jax.sharding import PartitionSpec as P

MESH = pl.DeviceIdType.MESH
BF16, F32 = jnp.bfloat16, jnp.float32

TILE = 128
Q_LOCAL, P_LOCAL, DEG = 8, 8, 12
NX, NZH, NZL, NY, NC = 4, 2, 4, 8, 2
PEERS = NY * NC
BLK = 4
HALF = 8
RUN = HALF * BLK
GROUP = RUN * P_LOCAL
PACK = P_LOCAL * BLK
GROUPS = NZL * PEERS // HALF
PLAN = ((3, (0, 1)), (2, (0, 1)), (1, (0, 1)), (0, (1,)), (0, (0,)))
CHUNKS = len(PLAN)
FIRST = [sum(len(c[1]) for c in PLAN[:n]) for n in range(CHUNKS)]


def remote(src, dst, send, recv, to):
    return pltpu.make_async_remote_copy(
        src_ref=src, dst_ref=dst, send_sem=send, recv_sem=recv, device_id=to, device_id_type=MESH
    )


def kernel(
    amp_hbm, mask_hbm, int_hbm, rows_hbm, slot_hbm, out, *scratch
):
    xs, amps, scratch = scratch[:CHUNKS], scratch[CHUNKS : 2 * CHUNKS], scratch[2 * CHUNKS :]
    lad, sent, got, mask, weights, rows, slot, turn, swap = scratch[:9]
    slot_wide, keeps, load_sem, gs, gr, ms, mr, met = scratch[9:]
    pair, virt = lax.axis_index("pair"), lax.axis_index("virt")
    zl, mine = pair // PEERS, lax.rem(pair, PEERS)
    y, core = mine // NC, lax.rem(mine, NC)
    zh, x = virt // NX, lax.rem(virt, NX)
    xr, xl, xo = lax.rem(x + 1, NX), lax.rem(x + 3, NX), lax.rem(x + 2, NX)
    zo = 1 - zh
    to_r, to_l, to_z = (pair, zh * NX + xr), (pair, zh * NX + xl), (pair, zo * NX + x)

    def flipped(k):
        return (zl, zl + 1 - 2 * lax.rem(zl, 2), lax.rem(zl + 2, 4), 3 - zl)[k]

    near = y // (NY // 2)

    def group_of(n, g):
        k, halves = PLAN[n]
        return flipped(k) * 2 + (near if halves[g] == 0 else 1 - near)

    def first_group(n):
        return group_of(n, 0) if len(PLAN[n][1]) == 1 else flipped(PLAN[n][0]) * 2

    def groups(n):
        return [first_group(n) + g for g in range(len(PLAN[n][1]))]

    def rows_of(n):
        size = RUN * len(PLAN[n][1])
        return pl.ds(pl.multiple_of(first_group(n) * RUN, RUN), size)

    barrier = pltpu.get_barrier_semaphore()
    y_peers = [(zl * PEERS + lax.rem(y + i, NY) * NC + core, virt) for i in range(1, NY)]
    z_peers = [
        (lax.rem(zl + i // NC, NZL) * PEERS + y * NC + lax.rem(core + i % NC, NC), virt)
        for i in range(1, NZL * NC)
    ]
    first = [to_r, to_l, to_z] + z_peers + y_peers
    for peer in first:
        pl.semaphore_signal(barrier, inc=1, device_id=peer, device_id_type=MESH)

    loads = [pltpu.make_async_copy(mask_hbm, mask, load_sem.at[0])]
    for n in range(CHUNKS):
        loads.append(pltpu.make_async_copy(amp_hbm.at[rows_of(n)], amps[n], load_sem.at[1 + n]))
    loads.append(pltpu.make_async_copy(slot_hbm, slot, load_sem.at[CHUNKS + 1]))
    loads.append(pltpu.make_async_copy(rows_hbm, rows, load_sem.at[CHUNKS + 2]))
    loads.append(pltpu.make_async_copy(int_hbm, weights, load_sem.at[CHUNKS + 3]))
    for load in loads:
        load.start()

    pending = []

    def gather(n, i, first_tile, tiles):
        block = xs[n].at[pl.ds(first_tile, tiles)]
        return block, gs.at[n, i], gr.at[n, i]

    def send(n, i, first_tile, tiles, to):
        block, s, r = gather(n, i, first_tile, tiles)
        copy = remote(block, block, s, r, to)
        copy.start()
        pending.append(copy)

    def arrived(n, i, first_tile, tiles):
        block, s, r = gather(n, i, first_tile, tiles)
        remote(block, block, s, r, to_z).wait_recv()

    def tile(z_hi, at_x):
        return (z_hi * NX + at_x) * Q_LOCAL

    own, other = tile(zh, x), tile(zo, x)

    def masked(n):
        loads[1 + n].wait()
        keep = keeps[rows_of(n), :]
        for q in range(Q_LOCAL):
            a = amps[n][:, q * TILE : (q + 1) * TILE].astype(F32)
            xs[n][own + q] = (a * keep[:, q : q + 1]).astype(BF16)

    loads[0].wait()
    keeps[...] = mask[...].astype(F32).T
    masked(0)
    pl.semaphore_wait(barrier, len(first))

    def own_x(n):
        send(n, 0, own, Q_LOCAL, to_r)
        send(n, 1, own, Q_LOCAL, to_l)

    def own_z(n):
        send(n, 2, own, Q_LOCAL, to_z)

    def pass_own(n):
        arrived(n, 0, tile(zh, xl), 8)
        send(n, 3, tile(zh, xl), 4, to_r)
        arrived(n, 1, tile(zh, xr), 8)
        send(n, 4, tile(zh, xr) + 4, 4, to_l)

    def cross(n):
        arrived(n, 2, other, 8)
        send(n, 5, other, 8, to_r)
        send(n, 6, other, 8, to_l)

    def forward(n):
        arrived(n, 5, tile(zo, xl), 8)
        send(n, 7, tile(zo, xl), 4, to_r)
        arrived(n, 6, tile(zo, xr), 8)
        send(n, 8, tile(zo, xr) + 4, 4, to_l)

    def complete(n):
        arrived(n, 3, tile(zh, xo), 4)
        arrived(n, 4, tile(zh, xo) + 4, 4)
        arrived(n, 7, tile(zo, xo), 4)
        arrived(n, 8, tile(zo, xo) + 4, 4)

    def work(n):
        complete(n)
        ladder(n)
        exchange(n)

    for n in range(CHUNKS):
        if n:
            masked(n)
        own_z(n)
        own_x(n)
    for peer in y_peers:
        pl.semaphore_signal(met, inc=1, device_id=peer, device_id_type=MESH)

    def grid(shape, axis):
        return lax.broadcasted_iota(jnp.int32, shape, axis)

    i, j = grid((GROUP, GROUP), 0), grid((GROUP, GROUP), 1)
    to_send = lax.rem(i // BLK, P_LOCAL) * (RUN) + (i // PACK) * BLK + lax.rem(i, BLK)
    turn[...] = jnp.where(j == to_send, 1.0, 0.0).astype(BF16)
    i, j = grid((TILE, TILE), 0), grid((TILE, TILE), 1)
    back = jnp.where(i + j == TILE - 1, 1.0, 0.0).astype(BF16)
    loads[CHUNKS + 1].wait()
    total = NZL * PEERS * BLK
    i, j = grid((total, NZL * PEERS), 0), grid((total, NZL * PEERS), 1)
    spread = jnp.where(i // BLK == j, 1.0, 0.0).astype(BF16)
    each = lax.dot_general(
        spread, slot[...].astype(F32).astype(BF16), (((1,), (1,)), ((), ())), preferred_element_type=F32
    )
    i, j = grid((total, BLK), 0), grid((total, BLK), 1)
    column = jnp.sum(jnp.where(lax.rem(i, BLK) == j, each, 0.0), axis=1, keepdims=True)
    slot_wide[...] = jnp.broadcast_to(column, (total, TILE))
    for n in range(CHUNKS):
        for g, group in enumerate(groups(n)):
            part = slot_wide[pl.ds(pl.multiple_of(group * RUN, RUN), RUN), :]
            for half in range(2):
                i, j = grid((RUN, TILE), 0), grid((RUN, TILE), 1)
                offset = (j + half * TILE - (i // BLK) * PACK).astype(F32) - part
                for p in range(P_LOCAL):
                    swap[FIRST[n] + g, p * RUN : (p + 1) * RUN, half * TILE : (half + 1) * TILE] = (
                        jnp.where(offset == float(p * BLK), 1.0, 0.0).astype(BF16)
                    )
    loads[CHUNKS + 2].wait()
    loads[CHUNKS + 3].wait()

    def ladder(n):
        size = len(PLAN[n][1])

        def one(p, carry):
            left = jnp.concatenate([xs[n][rows[p, k]] for k in range(DEG)], axis=1)
            acc = jnp.dot(left, weights[p], preferred_element_type=F32).astype(BF16)
            at = pl.ds(pl.multiple_of(p * RUN, RUN), RUN)
            for g in range(size):
                lad[FIRST[n] + g, at, :] = acc[g * RUN : (g + 1) * RUN]
            return carry

        lax.fori_loop(0, P_LOCAL, one, 0, unroll=8)
        for g in range(FIRST[n], FIRST[n] + size):
            packed = jnp.dot(turn[...], lad[g], preferred_element_type=F32).astype(BF16)
            sent[g * HALF : (g + 1) * HALF] = packed.reshape(HALF, PACK, TILE)

    def exchange(n):
        size, base = len(PLAN[n][1]) * HALF, FIRST[n] * HALF
        place = mine if size == PEERS else lax.rem(mine, HALF)
        own_group = PLAN[n][0] == 0 and 0 in PLAN[n][1]
        for i in range(1 if own_group else 0, size):
            at = lax.rem(place + i, size) if own_group else i
            peer = (first_group(n) * HALF + at, virt)
            remote(sent.at[base + at], got.at[base + place], ms.at[n], mr.at[n], peer).start()
        if own_group:
            got[base + place] = sent[base + place]

    def bytes_of(n):
        size, base = len(PLAN[n][1]) * HALF, FIRST[n] * HALF
        own_group = PLAN[n][0] == 0 and 0 in PLAN[n][1]
        part = pl.ds(base, size - 1 if own_group else size)
        return remote(sent.at[part], got.at[part], ms.at[n], mr.at[n], to_z)

    def combine(n):
        bytes_of(n).wait_recv()
        for g, group in enumerate(groups(n)):
            g += FIRST[n]
            block = got[g * HALF : (g + 1) * HALF].reshape(GROUP, TILE)
            mirrored = jnp.dot(swap[g], block, preferred_element_type=F32).astype(BF16)
            mirrored = jnp.dot(mirrored, back, preferred_element_type=F32)
            both = (lad[g].astype(F32) + mirrored).astype(BF16)
            start = pl.multiple_of(group * RUN, RUN)
            for p in range(P_LOCAL):
                out[pl.ds(start, RUN), p * TILE : (p + 1) * TILE] = both[p * RUN : (p + 1) * RUN]

    pl.semaphore_wait(met, len(y_peers))
    for step in range(CHUNKS + 4):
        if step < CHUNKS:
            pass_own(step)
        if 0 <= step - 1 < CHUNKS:
            cross(step - 1)
        if 0 <= step - 2 < CHUNKS:
            forward(step - 2)
        if 0 <= step - 3 < CHUNKS:
            work(step - 3)
    for copy in pending:
        copy.wait_send()
    for n in range(CHUNKS):
        combine(n)
    for n in range(CHUNKS):
        bytes_of(n).wait_send()


def on_device(amplitudes, amp_mask, integrals, int_rows, mirror_slot):
    hbm = pl.BlockSpec(memory_space=pl.ANY)
    total = NZL * PEERS * BLK
    return pl.pallas_call(
        kernel,
        out_shape=pltpu.VMEM((total, P_LOCAL * TILE), BF16),
        in_specs=[hbm] * 5,
        out_specs=pl.BlockSpec(memory_space=pltpu.VMEM),
        scratch_shapes=[pltpu.VMEM((NX * NZH * Q_LOCAL, RUN * len(c[1]), TILE), BF16) for c in PLAN]
        + [pltpu.VMEM((RUN * len(c[1]), Q_LOCAL * TILE), BF16) for c in PLAN]
        + [
            pltpu.VMEM((GROUPS, GROUP, TILE), BF16),
            pltpu.VMEM((GROUPS * HALF, PACK, TILE), BF16),
            pltpu.VMEM((GROUPS * HALF, PACK, TILE), BF16),
            pltpu.VMEM((Q_LOCAL, total), jnp.int32),
            pltpu.VMEM((P_LOCAL, DEG * TILE, TILE), BF16),
            pltpu.SMEM((P_LOCAL, DEG), jnp.int32),
            pltpu.VMEM((BLK, NZL * PEERS), jnp.int32),
            pltpu.VMEM((GROUP, GROUP), BF16),
            pltpu.VMEM((GROUPS, GROUP, GROUP), BF16),
            pltpu.VMEM((total, TILE), F32),
            pltpu.VMEM((total, Q_LOCAL), F32),
            pltpu.SemaphoreType.DMA((CHUNKS + 4,)),
            pltpu.SemaphoreType.DMA((CHUNKS, 9)),
            pltpu.SemaphoreType.DMA((CHUNKS, 9)),
            pltpu.SemaphoreType.DMA((CHUNKS,)),
            pltpu.SemaphoreType.DMA((CHUNKS,)),
            pltpu.SemaphoreType.REGULAR,
        ],
        compiler_params=pltpu.CompilerParams(
            collective_id=0, has_side_effects=True, vmem_limit_bytes=40 << 20
        ),
        name="ladder",
    )(
        *(
            pltpu.with_memory_space_constraint(a, pltpu.HBM)
            for a in (
                amplitudes,
                amp_mask.T,
                integrals.reshape(P_LOCAL, DEG * TILE, TILE),
                int_rows,
                mirror_slot.T,
            )
        )
    )


def solution(mesh):
    placed = (
        P("pair", "virt"),
        P("pair", "virt"),
        P("virt", None, None, None),
        P("virt", None),
        P("pair", None),
    )
    return jax.shard_map(
        on_device, mesh=mesh, in_specs=placed, out_specs=P("pair", "virt"), check_vma=False
    )
```

```python
import jax
import jax.numpy as jnp
from jax import lax
from jax.experimental import pallas as pl
from jax.experimental.pallas import tpu as pltpu
from jax.sharding import PartitionSpec as P

MESH = pl.DeviceIdType.MESH
BF16, F32 = jnp.bfloat16, jnp.float32

TILE = 128
Q_LOCAL, P_LOCAL, DEG = 8, 8, 12
NX, NZH, NZL, NY, NC = 4, 2, 4, 8, 2
PEERS = NY * NC
BLK = 4
HALF = 8
RUN = HALF * BLK
GROUP = RUN * P_LOCAL
PACK = P_LOCAL * BLK
GROUPS = NZL * PEERS // HALF
PLAN = ((2, (0, 1)), (3, (0, 1)), (1, (0, 1)), (0, (1,)), (0, (0,)))
CHUNKS = len(PLAN)
FIRST = [sum(len(c[1]) for c in PLAN[:n]) for n in range(CHUNKS)]


def remote(src, dst, send, recv, to):
    return pltpu.make_async_remote_copy(
        src_ref=src, dst_ref=dst, send_sem=send, recv_sem=recv, device_id=to, device_id_type=MESH
    )


def kernel(
    amp_hbm, mask_hbm, int_hbm, rows_hbm, slot_hbm, out, *scratch
):
    xs, amps, scratch = scratch[:CHUNKS], scratch[CHUNKS : 2 * CHUNKS], scratch[2 * CHUNKS :]
    lad, sent, got, mask, weights, rows, slot, turn, swap = scratch[:9]
    slot_wide, keeps, load_sem, gs, gr, ms, mr, met = scratch[9:]
    pair, virt = lax.axis_index("pair"), lax.axis_index("virt")
    zl, mine = pair // PEERS, lax.rem(pair, PEERS)
    y, core = mine // NC, lax.rem(mine, NC)
    zh, x = virt // NX, lax.rem(virt, NX)
    xr, xl, xo = lax.rem(x + 1, NX), lax.rem(x + 3, NX), lax.rem(x + 2, NX)
    zo = 1 - zh
    to_r, to_l, to_z = (pair, zh * NX + xr), (pair, zh * NX + xl), (pair, zo * NX + x)

    def flipped(k):
        return (zl, zl + 1 - 2 * lax.rem(zl, 2), lax.rem(zl + 2, 4), 3 - zl)[k]

    near = y // (NY // 2)

    def group_of(n, g):
        k, halves = PLAN[n]
        return flipped(k) * 2 + (near if halves[g] == 0 else 1 - near)

    def first_group(n):
        return group_of(n, 0) if len(PLAN[n][1]) == 1 else flipped(PLAN[n][0]) * 2

    def groups(n):
        return [first_group(n) + g for g in range(len(PLAN[n][1]))]

    def rows_of(n):
        size = RUN * len(PLAN[n][1])
        return pl.ds(pl.multiple_of(first_group(n) * RUN, RUN), size)

    barrier = pltpu.get_barrier_semaphore()
    y_peers = [(zl * PEERS + lax.rem(y + i, NY) * NC + core, virt) for i in range(1, NY)]
    z_peers = [
        (lax.rem(zl + i // NC, NZL) * PEERS + y * NC + lax.rem(core + i % NC, NC), virt)
        for i in range(1, NZL * NC)
    ]
    first = [to_r, to_l, to_z] + z_peers + y_peers
    for peer in first:
        pl.semaphore_signal(barrier, inc=1, device_id=peer, device_id_type=MESH)

    loads = [pltpu.make_async_copy(mask_hbm, mask, load_sem.at[0])]
    for n in range(CHUNKS):
        loads.append(pltpu.make_async_copy(amp_hbm.at[rows_of(n)], amps[n], load_sem.at[1 + n]))
    loads.append(pltpu.make_async_copy(slot_hbm, slot, load_sem.at[CHUNKS + 1]))
    loads.append(pltpu.make_async_copy(rows_hbm, rows, load_sem.at[CHUNKS + 2]))
    loads.append(pltpu.make_async_copy(int_hbm, weights, load_sem.at[CHUNKS + 3]))
    for load in loads:
        load.start()

    pending = []

    def gather(n, i, first_tile, tiles):
        block = xs[n].at[pl.ds(first_tile, tiles)]
        return block, gs.at[n, i], gr.at[n, i]

    def send(n, i, first_tile, tiles, to):
        block, s, r = gather(n, i, first_tile, tiles)
        copy = remote(block, block, s, r, to)
        copy.start()
        pending.append(copy)

    def arrived(n, i, first_tile, tiles):
        block, s, r = gather(n, i, first_tile, tiles)
        remote(block, block, s, r, to_z).wait_recv()

    def tile(z_hi, at_x):
        return (z_hi * NX + at_x) * Q_LOCAL

    own, other = tile(zh, x), tile(zo, x)

    def masked(n):
        loads[1 + n].wait()
        keep = keeps[rows_of(n), :]
        for q in range(Q_LOCAL):
            a = amps[n][:, q * TILE : (q + 1) * TILE].astype(F32)
            xs[n][own + q] = (a * keep[:, q : q + 1]).astype(BF16)

    loads[0].wait()
    keeps[...] = mask[...].astype(F32).T
    masked(0)
    pl.semaphore_wait(barrier, len(first))

    def own_x(n):
        send(n, 0, own, Q_LOCAL, to_r)
        send(n, 1, own, Q_LOCAL, to_l)

    def own_z(n):
        send(n, 2, own, Q_LOCAL, to_z)

    def pass_own(n):
        arrived(n, 0, tile(zh, xl), 8)
        send(n, 3, tile(zh, xl), 4, to_r)
        arrived(n, 1, tile(zh, xr), 8)
        send(n, 4, tile(zh, xr) + 4, 4, to_l)

    def cross(n):
        arrived(n, 2, other, 8)
        send(n, 5, other, 8, to_r)
        send(n, 6, other, 8, to_l)

    def forward(n):
        arrived(n, 5, tile(zo, xl), 8)
        send(n, 7, tile(zo, xl), 4, to_r)
        arrived(n, 6, tile(zo, xr), 8)
        send(n, 8, tile(zo, xr) + 4, 4, to_l)

    def complete(n):
        arrived(n, 3, tile(zh, xo), 4)
        arrived(n, 4, tile(zh, xo) + 4, 4)
        arrived(n, 7, tile(zo, xo), 4)
        arrived(n, 8, tile(zo, xo) + 4, 4)

    def work(n):
        complete(n)
        ladder(n)
        exchange(n)

    for n in range(CHUNKS):
        if n:
            masked(n)
        if n == 0:
            own_z(n)
        own_x(n)
    for peer in y_peers:
        pl.semaphore_signal(met, inc=1, device_id=peer, device_id_type=MESH)

    def grid(shape, axis):
        return lax.broadcasted_iota(jnp.int32, shape, axis)

    i, j = grid((GROUP, GROUP), 0), grid((GROUP, GROUP), 1)
    to_send = lax.rem(i // BLK, P_LOCAL) * (RUN) + (i // PACK) * BLK + lax.rem(i, BLK)
    turn[...] = jnp.where(j == to_send, 1.0, 0.0).astype(BF16)
    i, j = grid((TILE, TILE), 0), grid((TILE, TILE), 1)
    back = jnp.where(i + j == TILE - 1, 1.0, 0.0).astype(BF16)
    loads[CHUNKS + 1].wait()
    total = NZL * PEERS * BLK
    i, j = grid((total, NZL * PEERS), 0), grid((total, NZL * PEERS), 1)
    spread = jnp.where(i // BLK == j, 1.0, 0.0).astype(BF16)
    each = lax.dot_general(
        spread, slot[...].astype(F32).astype(BF16), (((1,), (1,)), ((), ())), preferred_element_type=F32
    )
    i, j = grid((total, BLK), 0), grid((total, BLK), 1)
    column = jnp.sum(jnp.where(lax.rem(i, BLK) == j, each, 0.0), axis=1, keepdims=True)
    slot_wide[...] = jnp.broadcast_to(column, (total, TILE))
    for n in range(CHUNKS):
        for g, group in enumerate(groups(n)):
            part = slot_wide[pl.ds(pl.multiple_of(group * RUN, RUN), RUN), :]
            for half in range(2):
                i, j = grid((RUN, TILE), 0), grid((RUN, TILE), 1)
                offset = (j + half * TILE - (i // BLK) * PACK).astype(F32) - part
                for p in range(P_LOCAL):
                    swap[FIRST[n] + g, p * RUN : (p + 1) * RUN, half * TILE : (half + 1) * TILE] = (
                        jnp.where(offset == float(p * BLK), 1.0, 0.0).astype(BF16)
                    )
    loads[CHUNKS + 2].wait()
    loads[CHUNKS + 3].wait()

    def ladder(n):
        size = len(PLAN[n][1])

        def one(p, carry):
            left = jnp.concatenate([xs[n][rows[p, k]] for k in range(DEG)], axis=1)
            acc = jnp.dot(left, weights[p], preferred_element_type=F32).astype(BF16)
            at = pl.ds(pl.multiple_of(p * RUN, RUN), RUN)
            for g in range(size):
                lad[FIRST[n] + g, at, :] = acc[g * RUN : (g + 1) * RUN]
            return carry

        lax.fori_loop(0, P_LOCAL, one, 0, unroll=8)
        for g in range(FIRST[n], FIRST[n] + size):
            packed = jnp.dot(turn[...], lad[g], preferred_element_type=F32).astype(BF16)
            sent[g * HALF : (g + 1) * HALF] = packed.reshape(HALF, PACK, TILE)

    def exchange(n):
        size, base = len(PLAN[n][1]) * HALF, FIRST[n] * HALF
        place = mine if size == PEERS else lax.rem(mine, HALF)
        own_group = PLAN[n][0] == 0 and 0 in PLAN[n][1]
        for i in range(1 if own_group else 0, size):
            at = lax.rem(place + i, size) if own_group else i
            peer = (first_group(n) * HALF + at, virt)
            remote(sent.at[base + at], got.at[base + place], ms.at[n], mr.at[n], peer).start()
        if own_group:
            got[base + place] = sent[base + place]

    def bytes_of(n):
        size, base = len(PLAN[n][1]) * HALF, FIRST[n] * HALF
        own_group = PLAN[n][0] == 0 and 0 in PLAN[n][1]
        part = pl.ds(base, size - 1 if own_group else size)
        return remote(sent.at[part], got.at[part], ms.at[n], mr.at[n], to_z)

    def combine(n):
        bytes_of(n).wait_recv()
        for g, group in enumerate(groups(n)):
            g += FIRST[n]
            block = got[g * HALF : (g + 1) * HALF].reshape(GROUP, TILE)
            mirrored = jnp.dot(swap[g], block, preferred_element_type=F32).astype(BF16)
            mirrored = jnp.dot(mirrored, back, preferred_element_type=F32)
            both = (lad[g].astype(F32) + mirrored).astype(BF16)
            start = pl.multiple_of(group * RUN, RUN)
            for p in range(P_LOCAL):
                out[pl.ds(start, RUN), p * TILE : (p + 1) * TILE] = both[p * RUN : (p + 1) * RUN]

    pl.semaphore_wait(met, len(y_peers))
    for step in range(CHUNKS + 4):
        if step < CHUNKS:
            if step + 1 < CHUNKS:
                own_z(step + 1)
            pass_own(step)
        if 0 <= step - 1 < CHUNKS:
            cross(step - 1)
        if 0 <= step - 2 < CHUNKS:
            forward(step - 2)
        if 0 <= step - 3 < CHUNKS:
            work(step - 3)
    for copy in pending:
        copy.wait_send()
    for n in range(CHUNKS):
        combine(n)
    for n in range(CHUNKS):
        bytes_of(n).wait_send()


def on_device(amplitudes, amp_mask, integrals, int_rows, mirror_slot):
    hbm = pl.BlockSpec(memory_space=pl.ANY)
    total = NZL * PEERS * BLK
    return pl.pallas_call(
        kernel,
        out_shape=pltpu.VMEM((total, P_LOCAL * TILE), BF16),
        in_specs=[hbm] * 5,
        out_specs=pl.BlockSpec(memory_space=pltpu.VMEM),
        scratch_shapes=[pltpu.VMEM((NX * NZH * Q_LOCAL, RUN * len(c[1]), TILE), BF16) for c in PLAN]
        + [pltpu.VMEM((RUN * len(c[1]), Q_LOCAL * TILE), BF16) for c in PLAN]
        + [
            pltpu.VMEM((GROUPS, GROUP, TILE), BF16),
            pltpu.VMEM((GROUPS * HALF, PACK, TILE), BF16),
            pltpu.VMEM((GROUPS * HALF, PACK, TILE), BF16),
            pltpu.VMEM((Q_LOCAL, total), jnp.int32),
            pltpu.VMEM((P_LOCAL, DEG * TILE, TILE), BF16),
            pltpu.SMEM((P_LOCAL, DEG), jnp.int32),
            pltpu.VMEM((BLK, NZL * PEERS), jnp.int32),
            pltpu.VMEM((GROUP, GROUP), BF16),
            pltpu.VMEM((GROUPS, GROUP, GROUP), BF16),
            pltpu.VMEM((total, TILE), F32),
            pltpu.VMEM((total, Q_LOCAL), F32),
            pltpu.SemaphoreType.DMA((CHUNKS + 4,)),
            pltpu.SemaphoreType.DMA((CHUNKS, 9)),
            pltpu.SemaphoreType.DMA((CHUNKS, 9)),
            pltpu.SemaphoreType.DMA((CHUNKS,)),
            pltpu.SemaphoreType.DMA((CHUNKS,)),
            pltpu.SemaphoreType.REGULAR,
        ],
        compiler_params=pltpu.CompilerParams(
            collective_id=0, has_side_effects=True, vmem_limit_bytes=40 << 20
        ),
        name="ladder",
    )(
        *(
            pltpu.with_memory_space_constraint(a, pltpu.HBM)
            for a in (
                amplitudes,
                amp_mask.T,
                integrals.reshape(P_LOCAL, DEG * TILE, TILE),
                int_rows,
                mirror_slot.T,
            )
        )
    )


def solution(mesh):
    placed = (
        P("pair", "virt"),
        P("pair", "virt"),
        P("virt", None, None, None),
        P("virt", None),
        P("pair", None),
    )
    return jax.shard_map(
        on_device, mesh=mesh, in_specs=placed, out_specs=P("pair", "virt"), check_vma=False
    )
```

```python
import jax
import jax.numpy as jnp
from jax import lax
from jax.experimental import pallas as pl
from jax.experimental.pallas import tpu as pltpu
from jax.sharding import PartitionSpec as P

MESH = pl.DeviceIdType.MESH
BF16, F32 = jnp.bfloat16, jnp.float32

TILE = 128
Q_LOCAL, P_LOCAL, DEG = 8, 8, 12
NX, NZH, NZL, NY, NC = 4, 2, 4, 8, 2
PEERS = NY * NC
BLK = 4
HALF = 8
RUN = HALF * BLK
GROUP = RUN * P_LOCAL
PACK = P_LOCAL * BLK
GROUPS = NZL * PEERS // HALF
PLAN = ((2, (0, 1)), (3, (0, 1)), (1, (0, 1)), (0, (1,)), (0, (0,)))
CHUNKS = len(PLAN)
FIRST = [sum(len(c[1]) for c in PLAN[:n]) for n in range(CHUNKS)]


def remote(src, dst, send, recv, to):
    return pltpu.make_async_remote_copy(
        src_ref=src, dst_ref=dst, send_sem=send, recv_sem=recv, device_id=to, device_id_type=MESH
    )


def kernel(
    amp_hbm, mask_hbm, int_hbm, rows_hbm, slot_hbm, out, *scratch
):
    xs, amps, scratch = scratch[:CHUNKS], scratch[CHUNKS : 2 * CHUNKS], scratch[2 * CHUNKS :]
    lad, sent, got, mask, weights, rows, slot, turn, swap = scratch[:9]
    slot_wide, keeps, load_sem, gs, gr, ms, mr, met = scratch[9:]
    pair, virt = lax.axis_index("pair"), lax.axis_index("virt")
    zl, mine = pair // PEERS, lax.rem(pair, PEERS)
    y, core = mine // NC, lax.rem(mine, NC)
    zh, x = virt // NX, lax.rem(virt, NX)
    xr, xl, xo = lax.rem(x + 1, NX), lax.rem(x + 3, NX), lax.rem(x + 2, NX)
    zo = 1 - zh
    to_r, to_l, to_z = (pair, zh * NX + xr), (pair, zh * NX + xl), (pair, zo * NX + x)

    def flipped(k):
        return (zl, zl + 1 - 2 * lax.rem(zl, 2), lax.rem(zl + 2, 4), 3 - zl)[k]

    near = y // (NY // 2)

    def group_of(n, g):
        k, halves = PLAN[n]
        return flipped(k) * 2 + (near if halves[g] == 0 else 1 - near)

    def first_group(n):
        return group_of(n, 0) if len(PLAN[n][1]) == 1 else flipped(PLAN[n][0]) * 2

    def groups(n):
        return [first_group(n) + g for g in range(len(PLAN[n][1]))]

    def rows_of(n):
        size = RUN * len(PLAN[n][1])
        return pl.ds(pl.multiple_of(first_group(n) * RUN, RUN), size)

    barrier = pltpu.get_barrier_semaphore()
    y_peers = [(zl * PEERS + lax.rem(y + i, NY) * NC + core, virt) for i in range(1, NY)]
    z_peers = [
        (lax.rem(zl + i // NC, NZL) * PEERS + y * NC + lax.rem(core + i % NC, NC), virt)
        for i in range(1, NZL * NC)
    ]
    first = [to_r, to_l, to_z] + z_peers + y_peers
    loads = [pltpu.make_async_copy(mask_hbm, mask, load_sem.at[0])]
    for n in range(CHUNKS):
        loads.append(pltpu.make_async_copy(amp_hbm.at[rows_of(n)], amps[n], load_sem.at[1 + n]))
    loads.append(pltpu.make_async_copy(slot_hbm, slot, load_sem.at[CHUNKS + 1]))
    loads.append(pltpu.make_async_copy(rows_hbm, rows, load_sem.at[CHUNKS + 2]))
    loads.append(pltpu.make_async_copy(int_hbm, weights, load_sem.at[CHUNKS + 3]))

    for load in loads[:3]:
        load.start()
    for peer in first:
        pl.semaphore_signal(barrier, inc=1, device_id=peer, device_id_type=MESH)

    for load in loads[3:]:
        load.start()
    pending = []

    def gather(n, i, first_tile, tiles):
        block = xs[n].at[pl.ds(first_tile, tiles)]
        return block, gs.at[n, i], gr.at[n, i]

    def send(n, i, first_tile, tiles, to):
        block, s, r = gather(n, i, first_tile, tiles)
        copy = remote(block, block, s, r, to)
        copy.start()
        pending.append(copy)

    def arrived(n, i, first_tile, tiles):
        block, s, r = gather(n, i, first_tile, tiles)
        remote(block, block, s, r, to_z).wait_recv()

    def tile(z_hi, at_x):
        return (z_hi * NX + at_x) * Q_LOCAL

    own, other = tile(zh, x), tile(zo, x)

    def masked(n):
        loads[1 + n].wait()
        keep = keeps[rows_of(n), :]
        for q in range(Q_LOCAL):
            a = amps[n][:, q * TILE : (q + 1) * TILE].astype(F32)
            xs[n][own + q] = (a * keep[:, q : q + 1]).astype(BF16)

    loads[0].wait()
    keeps[...] = mask[...].astype(F32).T
    masked(0)
    pl.semaphore_wait(barrier, len(first))

    def own_x(n):
        send(n, 0, own, Q_LOCAL, to_r)
        send(n, 1, own, Q_LOCAL, to_l)

    def own_z(n):
        send(n, 2, own, Q_LOCAL, to_z)

    def pass_own(n):
        arrived(n, 0, tile(zh, xl), 8)
        send(n, 3, tile(zh, xl), 4, to_r)
        arrived(n, 1, tile(zh, xr), 8)
        send(n, 4, tile(zh, xr) + 4, 4, to_l)

    def cross(n):
        arrived(n, 2, other, 8)
        send(n, 5, other, 8, to_r)
        send(n, 6, other, 8, to_l)

    def forward(n):
        arrived(n, 5, tile(zo, xl), 8)
        send(n, 7, tile(zo, xl), 4, to_r)
        arrived(n, 6, tile(zo, xr), 8)
        send(n, 8, tile(zo, xr) + 4, 4, to_l)

    def complete(n):
        arrived(n, 3, tile(zh, xo), 4)
        arrived(n, 4, tile(zh, xo) + 4, 4)
        arrived(n, 7, tile(zo, xo), 4)
        arrived(n, 8, tile(zo, xo) + 4, 4)

    def work(n):
        complete(n)
        ladder(n)
        exchange(n)

    for n in range(CHUNKS):
        if n:
            masked(n)
        if n == 0:
            own_z(n)
        own_x(n)
    for peer in y_peers:
        pl.semaphore_signal(met, inc=1, device_id=peer, device_id_type=MESH)

    def grid(shape, axis):
        return lax.broadcasted_iota(jnp.int32, shape, axis)

    i, j = grid((GROUP, GROUP), 0), grid((GROUP, GROUP), 1)
    to_send = lax.rem(i // BLK, P_LOCAL) * (RUN) + (i // PACK) * BLK + lax.rem(i, BLK)
    turn[...] = jnp.where(j == to_send, 1.0, 0.0).astype(BF16)
    i, j = grid((TILE, TILE), 0), grid((TILE, TILE), 1)
    back = jnp.where(i + j == TILE - 1, 1.0, 0.0).astype(BF16)
    loads[CHUNKS + 1].wait()
    total = NZL * PEERS * BLK
    i, j = grid((total, NZL * PEERS), 0), grid((total, NZL * PEERS), 1)
    spread = jnp.where(i // BLK == j, 1.0, 0.0).astype(BF16)
    each = lax.dot_general(
        spread, slot[...].astype(F32).astype(BF16), (((1,), (1,)), ((), ())), preferred_element_type=F32
    )
    i, j = grid((total, BLK), 0), grid((total, BLK), 1)
    column = jnp.sum(jnp.where(lax.rem(i, BLK) == j, each, 0.0), axis=1, keepdims=True)
    slot_wide[...] = jnp.broadcast_to(column, (total, TILE))
    for n in range(CHUNKS):
        for g, group in enumerate(groups(n)):
            part = slot_wide[pl.ds(pl.multiple_of(group * RUN, RUN), RUN), :]
            for half in range(2):
                i, j = grid((RUN, TILE), 0), grid((RUN, TILE), 1)
                offset = (j + half * TILE - (i // BLK) * PACK).astype(F32) - part
                for p in range(P_LOCAL):
                    swap[FIRST[n] + g, p * RUN : (p + 1) * RUN, half * TILE : (half + 1) * TILE] = (
                        jnp.where(offset == float(p * BLK), 1.0, 0.0).astype(BF16)
                    )
    loads[CHUNKS + 2].wait()
    loads[CHUNKS + 3].wait()

    def ladder(n):
        size = len(PLAN[n][1])

        def one(p, carry):
            left = jnp.concatenate([xs[n][rows[p, k]] for k in range(DEG)], axis=1)
            acc = jnp.dot(left, weights[p], preferred_element_type=F32).astype(BF16)
            at = pl.ds(pl.multiple_of(p * RUN, RUN), RUN)
            for g in range(size):
                lad[FIRST[n] + g, at, :] = acc[g * RUN : (g + 1) * RUN]
            return carry

        lax.fori_loop(0, P_LOCAL, one, 0, unroll=8)
        for g in range(FIRST[n], FIRST[n] + size):
            packed = jnp.dot(turn[...], lad[g], preferred_element_type=F32).astype(BF16)
            sent[g * HALF : (g + 1) * HALF] = packed.reshape(HALF, PACK, TILE)

    def exchange(n):
        size, base = len(PLAN[n][1]) * HALF, FIRST[n] * HALF
        place = mine if size == PEERS else lax.rem(mine, HALF)
        own_group = PLAN[n][0] == 0 and 0 in PLAN[n][1]
        for i in range(1 if own_group else 0, size):
            at = lax.rem(place + i, size) if own_group else i
            peer = (first_group(n) * HALF + at, virt)
            remote(sent.at[base + at], got.at[base + place], ms.at[n], mr.at[n], peer).start()
        if own_group:
            got[base + place] = sent[base + place]

    def bytes_of(n):
        size, base = len(PLAN[n][1]) * HALF, FIRST[n] * HALF
        own_group = PLAN[n][0] == 0 and 0 in PLAN[n][1]
        part = pl.ds(base, size - 1 if own_group else size)
        return remote(sent.at[part], got.at[part], ms.at[n], mr.at[n], to_z)

    def combine(n):
        bytes_of(n).wait_recv()
        for g, group in enumerate(groups(n)):
            g += FIRST[n]
            block = got[g * HALF : (g + 1) * HALF].reshape(GROUP, TILE)
            mirrored = jnp.dot(swap[g], block, preferred_element_type=F32).astype(BF16)
            mirrored = jnp.dot(mirrored, back, preferred_element_type=F32)
            both = (lad[g].astype(F32) + mirrored).astype(BF16)
            start = pl.multiple_of(group * RUN, RUN)
            for p in range(P_LOCAL):
                out[pl.ds(start, RUN), p * TILE : (p + 1) * TILE] = both[p * RUN : (p + 1) * RUN]

    pl.semaphore_wait(met, len(y_peers))
    for step in range(CHUNKS + 4):
        if step < CHUNKS:
            if step + 1 < CHUNKS:
                own_z(step + 1)
            pass_own(step)
        if 0 <= step - 1 < CHUNKS:
            cross(step - 1)
        if 0 <= step - 2 < CHUNKS:
            forward(step - 2)
        if 0 <= step - 3 < CHUNKS:
            work(step - 3)
    for copy in pending:
        copy.wait_send()
    for n in range(CHUNKS):
        combine(n)
    for n in range(CHUNKS):
        bytes_of(n).wait_send()


def on_device(amplitudes, amp_mask, integrals, int_rows, mirror_slot):
    hbm = pl.BlockSpec(memory_space=pl.ANY)
    total = NZL * PEERS * BLK
    return pl.pallas_call(
        kernel,
        out_shape=pltpu.VMEM((total, P_LOCAL * TILE), BF16),
        in_specs=[hbm] * 5,
        out_specs=pl.BlockSpec(memory_space=pltpu.VMEM),
        scratch_shapes=[pltpu.VMEM((NX * NZH * Q_LOCAL, RUN * len(c[1]), TILE), BF16) for c in PLAN]
        + [pltpu.VMEM((RUN * len(c[1]), Q_LOCAL * TILE), BF16) for c in PLAN]
        + [
            pltpu.VMEM((GROUPS, GROUP, TILE), BF16),
            pltpu.VMEM((GROUPS * HALF, PACK, TILE), BF16),
            pltpu.VMEM((GROUPS * HALF, PACK, TILE), BF16),
            pltpu.VMEM((Q_LOCAL, total), jnp.int32),
            pltpu.VMEM((P_LOCAL, DEG * TILE, TILE), BF16),
            pltpu.SMEM((P_LOCAL, DEG), jnp.int32),
            pltpu.VMEM((BLK, NZL * PEERS), jnp.int32),
            pltpu.VMEM((GROUP, GROUP), BF16),
            pltpu.VMEM((GROUPS, GROUP, GROUP), BF16),
            pltpu.VMEM((total, TILE), F32),
            pltpu.VMEM((total, Q_LOCAL), F32),
            pltpu.SemaphoreType.DMA((CHUNKS + 4,)),
            pltpu.SemaphoreType.DMA((CHUNKS, 9)),
            pltpu.SemaphoreType.DMA((CHUNKS, 9)),
            pltpu.SemaphoreType.DMA((CHUNKS,)),
            pltpu.SemaphoreType.DMA((CHUNKS,)),
            pltpu.SemaphoreType.REGULAR,
        ],
        compiler_params=pltpu.CompilerParams(
            collective_id=0, has_side_effects=True, vmem_limit_bytes=40 << 20
        ),
        name="ladder",
    )(
        *(
            pltpu.with_memory_space_constraint(a, pltpu.HBM)
            for a in (
                amplitudes,
                amp_mask.T,
                integrals.reshape(P_LOCAL, DEG * TILE, TILE),
                int_rows,
                mirror_slot.T,
            )
        )
    )


def solution(mesh):
    placed = (
        P("pair", "virt"),
        P("pair", "virt"),
        P("virt", None, None, None),
        P("virt", None),
        P("pair", None),
    )
    return jax.shard_map(
        on_device, mesh=mesh, in_specs=placed, out_specs=P("pair", "virt"), check_vma=False
    )
```
